128 devices in a mesh: row: 8 (over x, core), col: 16 (over z, y).
Axes of the slice: x: 4, y: 4, z: 4, core: 2. Of those that a mesh axis runs over, the one named last changes fastest.
Arguments:
- kernel: float32 [16, 8, 128, 8, 16, 128], P(None, 'row', None, None, 'col'), as said below
Outputs:
- factored: float32 [16, 8, 128, 8, 16, 128], P(None, 'row', None, None, 'col')
Inputs may be any that keep to these rules, and one draw needn't show every extreme that they name: kernel is symmetric and positive definite, with a diagonal that dominates in norm.
All inputs are finite; a program needn't handle non-finite values.
Results may differ from the reference program's by a relative error of at most 0.0001.
Values sent between devices are 32-bit elements; how exact they have to be, the bound alone decides.
No kernel may reach another device: no remote copies, remote signals or barrier semaphores. Data moves between devices by JAX's collectives and lax.ppermute only.
A program may use at most 128 MiB of HBM per device.

```python
import math
import jax
import jax.numpy as jnp
from jax import lax

NB = 128
RB = 16
CB = 8
N = 16384
N_ROW = 8
N_COL = 16


def draw_kernel(key, part):
    key = jax.random.fold_in(key, 11)
    first_key = jax.random.fold_in(key, 0)
    order = N
    panel_rows = 2 * NB
    raw_values = jax.random.normal(first_key, (order, order), jnp.float32)
    index = jnp.arange(order)
    symmetric = jnp.where(index[:, None] >= index[None, :], raw_values, raw_values.T)
    coupling = math.sqrt(order) / (math.sqrt(order) + math.sqrt(panel_rows)) ** 2 * 0.9
    cross_scale = math.sqrt(coupling * 4.5 * math.sqrt(panel_rows))
    inside = index < panel_rows
    same_side = inside[:, None] == inside[None, :]
    scaled = symmetric * jnp.where(same_side, 1.0, cross_scale)
    diag_add = jnp.where(inside, 4.5 * math.sqrt(panel_rows), 4.5 * math.sqrt(order))
    matrix = scaled + jnp.where(index[:, None] == index[None, :], diag_add[:, None], 0.0)
    return matrix.reshape(RB, N_ROW, NB, CB, N_COL, NB)


def setup_inputs(seed: int = 0) -> dict:
    key_of = jax.random.split(jax.random.key(seed), 2)
    kernel = draw_kernel(jax.random.fold_in(key_of[1], 71), 0)
    return dict(kernel=kernel)


def reference(kernel):
    order = kernel.shape[0] * kernel.shape[1] * kernel.shape[2]
    matrix = kernel.reshape(order, order)
    for k in range(2):
        s = k * NB
        e = s + NB
        diagonal = matrix[s:e, s:e]
        factor = jnp.linalg.cholesky(diagonal)
        identity = jnp.eye(NB, dtype=diagonal.dtype)
        inverse = lax.linalg.triangular_solve(factor, identity, left_side=True, lower=True)
        under_rows = jnp.dot(matrix[e:, s:e], inverse.T, precision=lax.Precision.HIGHEST)
        trailing = matrix[e:, e:] - jnp.dot(under_rows, under_rows.T, precision=lax.Precision.HIGHEST)
        matrix = matrix.at[e:, e:].set(trailing)
        matrix = matrix.at[s:e, s:e].set(factor)
        matrix = matrix.at[e:, s:e].set(under_rows)
        matrix = matrix.at[s:e, e:].set(jnp.zeros_like(matrix[s:e, e:]))
    return matrix.reshape(kernel.shape)
```

```python
import jax
import jax.numpy as jnp
from jax import lax
from jax.experimental import pallas as pl
from jax.experimental.pallas import tpu as pltpu
from jax.sharding import PartitionSpec as P

F32 = jnp.float32
BF16 = jnp.bfloat16
BOTH = ("row", "col")
NB = 128
W2 = 2 * NB
TR = 256


def split2(x):
    high = x.astype(BF16)
    return high, (x - high.astype(F32)).astype(BF16)


def factor_kernel(where_ref, mine_ref, other_ref, lower_ref, inverse_ref, s_ref):
    core = where_ref[0]
    size, sub_rows, group = W2, 8, 32

    def place(first, second):
        s_ref[0:NB, 0:NB] = first[0]
        s_ref[NB:W2, 0:NB] = second[0]
        s_ref[0:NB, NB:W2] = second[0].T
        s_ref[NB:W2, NB:W2] = second[1]

    @pl.when(core == 0)
    def _():
        place(mine_ref, other_ref)

    @pl.when(core == 1)
    def _():
        place(other_ref, mine_ref)

    rows = lax.broadcasted_iota(jnp.int32, (size, size), 0)
    cols = lax.broadcasted_iota(jnp.int32, (size, size), 1)
    s_ref[:, size:] = jnp.where(rows == cols, 1.0, 0.0)
    sub = lax.broadcasted_iota(jnp.int32, (sub_rows, NB), 0)
    tiles = 3
    width = NB * tiles
    panels = group // sub_rows
    for o in range(0, size, group):
        lo = (o // NB) * NB
        r = [
            [
                s_ref[o + sub_rows * q : o + sub_rows * (q + 1), lo + NB * t : lo + NB * (t + 1)]
                for t in range(tiles)
            ]
            for q in range(panels)
        ]
        for p in range(panels):
            oo = o - lo + p * sub_rows
            c = [
                [jnp.broadcast_to(r[q][0][:, oo + j : oo + j + 1], (sub_rows, NB)) for j in range(sub_rows)]
                if q >= p
                else None
                for q in range(panels)
            ]
            b = [
                [
                    jnp.broadcast_to(c[p][j][i : i + 1, :], (sub_rows, NB)) if i >= j else None
                    for j in range(sub_rows)
                ]
                for i in range(sub_rows)
            ]
            scale = None
            for k in range(sub_rows):
                s = lax.rsqrt(b[k][k])
                scale = s if scale is None else jnp.where(sub >= k, s, scale)
                m = [None] * sub_rows
                for i in range(k + 1, sub_rows):
                    m[i] = b[i][k] * s
                for i in range(k + 1, sub_rows):
                    for j in range(k + 1, i + 1):
                        b[i][j] = b[i][j] - m[i] * m[j]
                u = [jnp.broadcast_to(r[p][t][k : k + 1, :], (sub_rows, NB)) * s for t in range(tiles)]
                for q in range(p, panels):
                    mult = c[q][k] * s
                    for j in range(k + 1, sub_rows):
                        c[q][j] = c[q][j] - mult * m[j]
                    if q == p:
                        if k == sub_rows - 1:
                            continue
                        mult = jnp.where(sub > k, mult, 0.0)
                    r[q] = [r[q][t] - mult * u[t] for t in range(tiles)]
            for t in range(tiles):
                s_ref[
                    o + sub_rows * p : o + sub_rows * (p + 1), lo + NB * t : lo + NB * (t + 1)
                ] = r[p][t] * scale
        if o + group < size:
            lo2 = ((o + group) // NB) * NB
            uu = s_ref[o : o + group, lo2 : lo + width]
            left = size - lo2
            h = uu.astype(BF16).astype(F32)
            rest = uu - h
            mid = rest.astype(BF16).astype(F32)
            low = rest - mid
            lhs = jnp.concatenate([h, h, mid, h, low, mid], axis=0)[:, :left].astype(BF16)
            rhs = jnp.concatenate([h, mid, h, low, h, mid], axis=0).astype(BF16)
            update = lax.dot_general(lhs, rhs, (((0,), (0,)), ((), ())), preferred_element_type=F32)
            skip = o + group - lo2
            s_ref[o + group : size, lo2 : lo + width] = (
                s_ref[o + group : size, lo2 : lo + width] - update[skip:, :]
            )
    lower_ref[...] = jnp.where(cols >= rows, s_ref[:, 0:size], 0.0).T
    inverse_ref[...] = jnp.where(cols <= rows, s_ref[:, size:], 0.0)


def factor_corner(place, mine, other):
    vmem = pl.BlockSpec(memory_space=pltpu.VMEM)
    return pl.pallas_call(
        factor_kernel,
        out_shape=(jax.ShapeDtypeStruct((W2, W2), F32),) * 2,
        in_specs=[pl.BlockSpec(memory_space=pltpu.SMEM), vmem, vmem],
        out_specs=(vmem, vmem),
        scratch_shapes=[pltpu.VMEM((W2, 2 * W2), F32)],
        compiler_params=pltpu.CompilerParams(vmem_limit_bytes=8 * 1024 * 1024),
        cost_estimate=pl.CostEstimate(flops=20_000_000, bytes_accessed=1_000_000, transcendentals=256),
        name="corner_factor",
    )(place, mine, other)


def trailing_kernel(
    place_ref, lower_ref, inverse_ref, g_ref, gp_ref, gm_ref, rp_ref, rm_ref, cmine_ref, cother_ref, m_ref,
    o_ref, a_ref, lt_ref, wc_ref, sems,
):
    step = pl.program_id(0)
    row, col, core, z, y = (place_ref[n] for n in range(5))

    @pl.when(step == 0)
    def _():
        copies = [
            pltpu.make_async_copy(src, dst, sems.at[n])
            for n, (src, dst) in enumerate(
                [
                    (g_ref, a_ref.at[0:4]),
                    (gm_ref, a_ref.at[4:8]),
                    (rp_ref, a_ref.at[8:10]),
                    (rm_ref, a_ref.at[10:12]),
                    (gp_ref, a_ref.at[12:16]),
                ]
            )
        ]
        for copy in copies:
            copy.start()
        inverse = inverse_ref[...]
        high, low = split2(inverse.T)
        lt_ref[0:W2, :] = high
        lt_ref[W2 : 2 * W2, :] = low
        lt_ref[2 * W2 : 3 * W2, :] = high
        high, low = split2(inverse)
        lhs = jnp.concatenate([high, high, low], axis=1)

        def columns(first, second):
            for j in range(0, 8, 2):
                x = jnp.concatenate(
                    [
                        jnp.concatenate([ref[:, jj, :] for ref in (first, second)], axis=0)
                        for jj in (j, j + 1)
                    ],
                    axis=1,
                )
                xh, xl = split2(x)
                w = jnp.dot(lhs, jnp.concatenate([xh, xl, xh], axis=0), preferred_element_type=F32)
                wh, wl = split2(w)
                span = pl.ds(j * NB, W2)
                wc_ref[0:W2, span] = wh
                wc_ref[W2 : 2 * W2, span] = wl
                wc_ref[2 * W2 : 3 * W2, span] = wh

        @pl.when(core == 0)
        def _():
            columns(cmine_ref, cother_ref)

        @pl.when(core == 1)
        def _():
            columns(cother_ref, cmine_ref)

        for copy in copies:
            copy.wait()

    half = step // 4
    zfirst = ((step // 2 - z + 4) % 4) * 4 + step % 2
    unit0 = jnp.where(core == 0, zfirst, ((3 * half - y + 4) % 4) * 4 + step % 4)
    unit1 = jnp.where(core == 0, zfirst + 2, ((1 + half - y + 4) % 4) * 4 + step % 4)
    a = jnp.concatenate([a_ref[unit0], a_ref[unit1]], axis=1)
    ah, al = split2(a)
    w = jnp.dot(jnp.concatenate([ah, ah, al], axis=1), lt_ref[...], preferred_element_type=F32)
    wh, wl = split2(w)
    u = jnp.dot(jnp.concatenate([wh, wh, wl], axis=1), wc_ref[...], preferred_element_type=F32)
    o_ref[...] = m_ref[...] - u.reshape(TR, 8, NB)

    @pl.when(col == 0)
    def _():
        o_ref[:, 0, :] = w[:, 0:NB]

    @pl.when(col == 1)
    def _():
        o_ref[:, 0, :] = w[:, NB:W2]

    @pl.when((step == 0) & (row < 2))
    def _():
        o_ref[0:NB, :, :] = jnp.zeros((NB, 8, NB), F32)

        @pl.when(col < 2)
        def _():
            o_ref[0:NB, 0, :] = lower_ref[
                pl.ds(pl.multiple_of(row * NB, NB), NB), pl.ds(pl.multiple_of(col * NB, NB), NB)
            ]


def update_trailing(place, lower, inverse, g, gp, gm, rp, rm, cmine, cother, m):
    anywhere = pl.BlockSpec(memory_space=pl.ANY)
    whole = lambda shape: pl.BlockSpec(shape, lambda i: (0,) * len(shape))
    rows = m.shape[0]
    block = pl.BlockSpec((TR, 8, NB), lambda i: (i, 0, 0))
    return pl.pallas_call(
        trailing_kernel,
        grid=(rows // TR,),
        out_shape=jax.ShapeDtypeStruct(m.shape, F32),
        in_specs=[
            pl.BlockSpec(memory_space=pltpu.SMEM),
            whole((W2, W2)),
            whole((W2, W2)),
            anywhere,
            anywhere,
            anywhere,
            anywhere,
            anywhere,
            whole((NB, 8, NB)),
            whole((NB, 8, NB)),
            block,
        ],
        out_specs=block,
        scratch_shapes=[
            pltpu.VMEM((16, TR, NB), F32),
            pltpu.VMEM((3 * W2, W2), BF16),
            pltpu.VMEM((3 * W2, 8 * NB), BF16),
            pltpu.SemaphoreType.DMA((5,)),
        ],
        compiler_params=pltpu.CompilerParams(vmem_limit_bytes=32 * 1024 * 1024),
        cost_estimate=pl.CostEstimate(flops=4_000_000_000, bytes_accessed=20_000_000, transcendentals=0),
        name="trailing_update",
    )(place, lower, inverse, g, gp, gm, rp, rm, cmine, cother, m)


def device(x, core, z, y):
    return (x % 4 * 2 + core) * 16 + z % 4 * 4 + y % 4


def pairs(moves):
    return [(device(*a), device(*b)) for a, b in moves]


SPAN = range(4)
CORES = range(2)


def along_x(hops):
    return pairs(
        [((a, k, z, y), (b, k, z, y)) for a, b in hops for k in CORES for z in SPAN for y in SPAN]
    )


def along_z(hops, cores=CORES, ys=SPAN):
    return [((x, k, a, y), (x, k, b, y)) for a, b in hops for x in SPAN for k in cores for y in ys]


def along_y(hops, cores=CORES, zs=SPAN):
    return [((x, k, z, a), (x, k, z, b)) for a, b in hops for x in SPAN for k in cores for z in zs]


SWAP = pairs([((x, k, z, y), (x, 1 - k, z, y)) for x in SPAN for k in CORES for z in SPAN for y in SPAN])


def send(value, moves):
    return lax.ppermute(value, BOTH, moves)


def spread_corner(block, x, z, y):
    e = jnp.where((x == 0) & (z == 0) & (y < 2), block, 0.0)
    e = e + send(e, along_x([(0, 1)]))
    e = e + send(e, along_x([(0, 3), (1, 2)]))
    e = e + send(e, pairs(along_z([(0, 1)])))
    e = e + send(e, pairs(along_z([(0, 3), (1, 2)])))
    f = send(e, pairs(along_y([(0, 1), (1, 0)])))
    two = jnp.where(y == 0, jnp.stack([e, f]), jnp.stack([f, e]))
    two = jnp.where(y < 2, two, 0.0)
    return two + send(two, pairs(along_y([(0, 3), (1, 2)])))


def spread_rows(units, core, z, y):
    first = core == 0
    lone = lax.dynamic_slice_in_dim(units, 2 + 2 * core, 2, 0)
    split_y = along_y([(0, 3), (1, 2)], cores=(1,), zs=(0,))
    r1 = send(lone, pairs(along_z([(0, 1)], cores=(0,), ys=(0, 1)) + split_y))
    r2 = send(units[6:8], pairs(along_z([(0, 3)], cores=(0,), ys=(0, 1)) + split_y))
    r3 = send(units[4:6], pairs(along_z([(0, 2)], cores=(0,), ys=(0, 1))))
    kept = jnp.where(first, z == 0, y < 2)
    r_all = r1 + r2 + r3
    x0 = jnp.where(kept, units[0:2], jnp.where(first, r_all, r1))
    x1 = jnp.where(first, x0, jnp.where(kept, units[2:4], r2))
    own = jnp.concatenate([x0, x1])
    up = [(a, a + 1) for a in SPAN]
    down = [(a, a - 1) for a in SPAN]
    bp = send(own, pairs(along_y([(0, 1), (1, 2)], cores=(0,)) + along_z([(0, 1)], cores=(1,))))
    bm = send(own, pairs(along_y([(0, 3), (1, 0)], cores=(0,)) + along_z([(0, 3)], cores=(1,))))
    rp = send(bp[0:2], pairs(along_y([(1, 2), (2, 3)], cores=(0,)) + along_z([(1, 2)], cores=(1,))))
    rm = send(bm[2:4], pairs(along_z([(3, 2)], cores=(1,))))
    at = jnp.where(first, y, z)
    g0 = jnp.where(
        first,
        lax.select_n(at, own[0:2], bp[0:2], rp, bm[0:2]),
        lax.select_n(at, own[0:2], bp[0:2], rp, bm[0:2]),
    )
    g1 = lax.select_n(
        jnp.where(first, at, at + 4),
        bm[2:4], own[2:4], bp[2:4], rp,
        own[2:4], bp[2:4], rm, bm[2:4],
    )
    g = jnp.concatenate([g0, g1])
    ahead = pairs(along_z(up, cores=(0,)) + along_y(up, cores=(1,)))
    back = pairs(along_z(down, cores=(0,)) + along_y(down, cores=(1,)))
    gp = send(g, ahead)
    gm = send(g, back)
    return g, gp, gm, send(gp[0:2], ahead), send(gm[2:4], back)


def local(kernel):
    row = lax.axis_index("row")
    col = lax.axis_index("col")
    x, core, z, y = row // 2, row % 2, col // 4, col % 4
    place = jnp.stack([row, col, core, z, y]).astype(jnp.int32)
    m = kernel.reshape(16 * NB, 8, NB)
    top = m[0:NB]
    mine = spread_corner(top[:, 0, :], x, z, y)
    other = send(mine, SWAP)
    lower, inverse = factor_corner(place[2:3], mine, other)
    pieces = spread_rows(m[:, 0, :].reshape(8, TR, NB), core, z, y)
    c = jnp.where(
        x == 0,
        top,
        send(top, along_x([(0, 1)])) + send(top, along_x([(0, 3)])) + send(top, along_x([(0, 2)])),
    )
    result = update_trailing(place, lower, inverse, *pieces, c, send(c, SWAP), m)
    return result.reshape(kernel.shape)


def solution(mesh):
    placed = P(None, "row", None, None, "col", None)
    return jax.shard_map(local, mesh=mesh, in_specs=(placed,), out_specs=placed, check_vma=False)
```

```python
import jax
import jax.numpy as jnp
from jax import lax
from jax.experimental import pallas as pl
from jax.experimental.pallas import tpu as pltpu
from jax.sharding import PartitionSpec as P

F32 = jnp.float32
BF16 = jnp.bfloat16
BOTH = ("row", "col")
NB = 128
W2 = 2 * NB
TR = 256


def split2(x):
    high = x.astype(BF16)
    return high, (x - high.astype(F32)).astype(BF16)


def factor_kernel(where_ref, mine_ref, other_ref, lower_ref, inverse_ref, s_ref):
    core = where_ref[0]
    size, sub_rows, group = W2, 8, 32

    def place(first, second):
        s_ref[0:NB, 0:NB] = first[0]
        s_ref[NB:W2, 0:NB] = second[0]
        s_ref[0:NB, NB:W2] = second[0].T
        s_ref[NB:W2, NB:W2] = second[1]

    @pl.when(core == 0)
    def _():
        place(mine_ref, other_ref)

    @pl.when(core == 1)
    def _():
        place(other_ref, mine_ref)

    rows = lax.broadcasted_iota(jnp.int32, (size, size), 0)
    cols = lax.broadcasted_iota(jnp.int32, (size, size), 1)
    s_ref[:, size:] = jnp.where(rows == cols, 1.0, 0.0)
    sub = lax.broadcasted_iota(jnp.int32, (sub_rows, NB), 0)
    tiles = 3
    width = NB * tiles
    panels = group // sub_rows
    for o in range(0, size, group):
        lo = (o // NB) * NB
        r = [
            [
                s_ref[o + sub_rows * q : o + sub_rows * (q + 1), lo + NB * t : lo + NB * (t + 1)]
                for t in range(tiles)
            ]
            for q in range(panels)
        ]
        for p in range(panels):
            oo = o - lo + p * sub_rows
            c = [
                [jnp.broadcast_to(r[q][0][:, oo + j : oo + j + 1], (sub_rows, NB)) for j in range(sub_rows)]
                if q >= p
                else None
                for q in range(panels)
            ]
            b = [
                [
                    jnp.broadcast_to(c[p][j][i : i + 1, :], (sub_rows, NB)) if i >= j else None
                    for j in range(sub_rows)
                ]
                for i in range(sub_rows)
            ]
            scale = None
            for k in range(sub_rows):
                s = lax.rsqrt(b[k][k])
                scale = s if scale is None else jnp.where(sub >= k, s, scale)
                m = [None] * sub_rows
                for i in range(k + 1, sub_rows):
                    m[i] = b[i][k] * s
                for i in range(k + 1, sub_rows):
                    for j in range(k + 1, i + 1):
                        b[i][j] = b[i][j] - m[i] * m[j]
                u = [jnp.broadcast_to(r[p][t][k : k + 1, :], (sub_rows, NB)) * s for t in range(tiles)]
                for q in range(p, panels):
                    mult = c[q][k] * s
                    for j in range(k + 1, sub_rows):
                        c[q][j] = c[q][j] - mult * m[j]
                    if q == p:
                        if k == sub_rows - 1:
                            continue
                        mult = jnp.where(sub > k, mult, 0.0)
                    r[q] = [r[q][t] - mult * u[t] for t in range(tiles)]
            for t in range(tiles):
                s_ref[
                    o + sub_rows * p : o + sub_rows * (p + 1), lo + NB * t : lo + NB * (t + 1)
                ] = r[p][t] * scale
        if o + group < size:
            lo2 = ((o + group) // NB) * NB
            uu = s_ref[o : o + group, lo2 : lo + width]
            left = size - lo2
            h = uu.astype(BF16).astype(F32)
            rest = uu - h
            mid = rest.astype(BF16).astype(F32)
            low = rest - mid
            lhs = jnp.concatenate([h, h, mid, h, low, mid], axis=0)[:, :left].astype(BF16)
            rhs = jnp.concatenate([h, mid, h, low, h, mid], axis=0).astype(BF16)
            update = lax.dot_general(lhs, rhs, (((0,), (0,)), ((), ())), preferred_element_type=F32)
            skip = o + group - lo2
            s_ref[o + group : size, lo2 : lo + width] = (
                s_ref[o + group : size, lo2 : lo + width] - update[skip:, :]
            )
    lower_ref[...] = jnp.where(cols >= rows, s_ref[:, 0:size], 0.0).T
    inverse_ref[...] = jnp.where(cols <= rows, s_ref[:, size:], 0.0)


def factor_corner(place, mine, other):
    vmem = pl.BlockSpec(memory_space=pltpu.VMEM)
    return pl.pallas_call(
        factor_kernel,
        out_shape=(jax.ShapeDtypeStruct((W2, W2), F32),) * 2,
        in_specs=[pl.BlockSpec(memory_space=pltpu.SMEM), vmem, vmem],
        out_specs=(vmem, vmem),
        scratch_shapes=[pltpu.VMEM((W2, 2 * W2), F32)],
        compiler_params=pltpu.CompilerParams(vmem_limit_bytes=8 * 1024 * 1024),
        cost_estimate=pl.CostEstimate(flops=8_000_000_000, bytes_accessed=1_000_000, transcendentals=256),
        name="corner_factor",
    )(place, mine, other)


STEPS = 8


def trailing_kernel(
    place_ref, lower_ref, inverse_ref, g_ref, gm_ref, gf_ref, gp_ref, columns_ref, m_ref,
    o_ref, a_ref, old_ref, new_ref, wc_ref, a_sems, m_sems, o_sems,
):
    row, col, core, z, y = (place_ref[n] for n in range(5))
    here = jnp.where(core == 0, z, y)
    pieces = [
        pltpu.make_async_copy(ref, a_ref.at[n], a_sems.at[n])
        for n, ref in enumerate((g_ref, gm_ref, gf_ref, gp_ref))
    ]
    for piece in pieces:
        piece.start()
    loads = [
        pltpu.make_async_copy(
            m_ref.at[s * TR : (s + 1) * TR], old_ref.at[s], m_sems.at[s]
        )
        for s in range(STEPS)
    ]
    for load in loads:
        load.start()

    inverse = inverse_ref[...]
    high, low = split2(inverse.T)
    lt = jnp.concatenate([high, low, high], axis=0)
    high, low = split2(inverse)
    lhs = jnp.concatenate([high, high, low], axis=1)
    for j in range(0, 8, 2):
        x = jnp.concatenate(
            [
                jnp.concatenate([columns_ref[n, :, jj, :] for n in range(2)], axis=0)
                for jj in (j, j + 1)
            ],
            axis=1,
        )
        xh, xl = split2(x)
        w = jnp.dot(lhs, jnp.concatenate([xh, xl, xh], axis=0), preferred_element_type=F32)
        wh, wl = split2(w)
        span = pl.ds(j * NB, W2)
        wc_ref[0:W2, span] = wh
        wc_ref[W2 : 2 * W2, span] = wl
        wc_ref[2 * W2 : 3 * W2, span] = wh
    for piece in pieces:
        piece.wait()

    stores = []
    for s in range(STEPS):
        half = s // 4
        slot0 = (jnp.where(core == 0, half, 3 * half) - here + 4) % 4
        slot1 = (jnp.where(core == 0, 2 + half, 1 + half) - here + 4) % 4
        a = jnp.concatenate([a_ref[slot0, s % 4], a_ref[slot1, s % 4]], axis=1)
        ah, al = split2(a)
        w = jnp.dot(jnp.concatenate([ah, ah, al], axis=1), lt, preferred_element_type=F32)
        wh, wl = split2(w)
        u = jnp.dot(jnp.concatenate([wh, wh, wl], axis=1), wc_ref[...], preferred_element_type=F32)
        loads[s].wait()
        new_ref[s] = old_ref[s] - u.reshape(TR, 8, NB)

        @pl.when(col == 0)
        def _():
            new_ref[s, :, 0, :] = w[:, 0:NB]

        @pl.when(col == 1)
        def _():
            new_ref[s, :, 0, :] = w[:, NB:W2]

        if s == 0:

            @pl.when(row < 2)
            def _():
                new_ref[s, 0:NB, :, :] = jnp.zeros((NB, 8, NB), F32)

                @pl.when(col < 2)
                def _():
                    new_ref[s, 0:NB, 0, :] = lower_ref[
                        pl.ds(pl.multiple_of(row * NB, NB), NB), pl.ds(pl.multiple_of(col * NB, NB), NB)
                    ]

        store = pltpu.make_async_copy(
            new_ref.at[s], o_ref.at[s * TR : (s + 1) * TR], o_sems.at[s]
        )
        store.start()
        stores.append(store)
    for store in stores:
        store.wait()


def update_trailing(place, lower, inverse, pieces, columns, m):
    anywhere = pl.BlockSpec(memory_space=pl.ANY)
    vmem = pl.BlockSpec(memory_space=pltpu.VMEM)
    return pl.pallas_call(
        trailing_kernel,
        out_shape=jax.ShapeDtypeStruct(m.shape, F32),
        in_specs=[pl.BlockSpec(memory_space=pltpu.SMEM), vmem, vmem] + [anywhere] * 4 + [vmem, anywhere],
        out_specs=anywhere,
        scratch_shapes=[
            pltpu.VMEM((4, 4, TR, NB), F32),
            pltpu.VMEM((STEPS, TR, 8, NB), F32),
            pltpu.VMEM((STEPS, TR, 8, NB), F32),
            pltpu.VMEM((3 * W2, 8 * NB), BF16),
            pltpu.SemaphoreType.DMA((4,)),
            pltpu.SemaphoreType.DMA((STEPS,)),
            pltpu.SemaphoreType.DMA((STEPS,)),
        ],
        compiler_params=pltpu.CompilerParams(vmem_limit_bytes=36 * 1024 * 1024),
        cost_estimate=pl.CostEstimate(flops=4_000_000_000, bytes_accessed=20_000_000, transcendentals=0),
        name="trailing_update",
    )(place, lower, inverse, *pieces, columns, m)


def device(x, core, z, y):
    return (x % 4 * 2 + core) * 16 + z % 4 * 4 + y % 4


def pairs(moves):
    return [(device(*a), device(*b)) for a, b in moves]


SPAN = range(4)
CORES = range(2)


def along_x(hops):
    return pairs(
        [((a, k, z, y), (b, k, z, y)) for a, b in hops for k in CORES for z in SPAN for y in SPAN]
    )


def along_z(hops, cores=CORES, ys=SPAN, xs=SPAN):
    return [((x, k, a, y), (x, k, b, y)) for a, b in hops for x in xs for k in cores for y in ys]


def along_y(hops, cores=CORES, zs=SPAN, xs=SPAN):
    return [((x, k, z, a), (x, k, z, b)) for a, b in hops for x in xs for k in cores for z in zs]


SWAP = pairs([((x, k, z, y), (x, 1 - k, z, y)) for x in SPAN for k in CORES for z in SPAN for y in SPAN])


def send(value, moves):
    return lax.ppermute(value, BOTH, moves)


def after(value, *others):
    return lax.optimization_barrier((value, *others))[0]


def extract_kernel(place_ref, m_ref, first_ref, second_ref, block_ref, top_ref, sems):
    x, z, y = (place_ref[n] for n in (5, 3, 4))
    top = pltpu.make_async_copy(m_ref.at[0:NB], top_ref, sems.at[9])
    block = pltpu.make_async_copy(m_ref.at[0:NB, 0, :], block_ref, sems.at[8])
    source = (z == 0) & (y < 2)
    corner = source & (x == 0)

    @pl.when(x == 0)
    def _():
        top.start()

    @pl.when(corner)
    def _():
        block.start()

    @pl.when(source)
    def _():
        copies = [
            pltpu.make_async_copy(m_ref.at[TR * n : TR * (n + 1), 0, :], ref.at[n % 4], sems.at[n])
            for n, ref in enumerate([first_ref] * 4 + [second_ref] * 4)
        ]
        for copy in copies:
            copy.start()
        for copy in copies:
            copy.wait()

    @pl.when(corner)
    def _():
        block.wait()

    @pl.when(jnp.logical_not(corner))
    def _():
        block_ref[...] = jnp.zeros((NB, NB), F32)

    @pl.when(x == 0)
    def _():
        top.wait()


def extract(place, m):
    anywhere = pl.BlockSpec(memory_space=pl.ANY)
    half = jax.ShapeDtypeStruct((4, TR, NB), F32)
    return pl.pallas_call(
        extract_kernel,
        out_shape=(half, half, jax.ShapeDtypeStruct((NB, NB), F32), jax.ShapeDtypeStruct((NB, 8, NB), F32)),
        in_specs=[pl.BlockSpec(memory_space=pltpu.SMEM), anywhere],
        out_specs=(anywhere, anywhere, pl.BlockSpec(memory_space=pltpu.VMEM), anywhere),
        scratch_shapes=[pltpu.SemaphoreType.DMA((10,))],
        compiler_params=pltpu.CompilerParams(vmem_limit_bytes=4 * 1024 * 1024),
        cost_estimate=pl.CostEstimate(flops=0, bytes_accessed=4_000_000, transcendentals=0),
        name="extract_panels",
    )(place, m)


def local(kernel):
    row = lax.axis_index("row")
    col = lax.axis_index("col")
    x, core, z, y = row // 2, row % 2, col // 4, col % 4
    place = jnp.stack([row, col, core, z, y, x]).astype(jnp.int32)
    m = kernel.reshape(16 * NB, 8, NB)
    m = pltpu.with_memory_space_constraint(m, pltpu.HBM)
    first, second, e, top = extract(place, m)

    plane = (0,)
    f = send(e, pairs(along_y([(0, 1), (1, 0)], xs=plane, zs=(0,))))

    lay_y = along_y([(0, 3), (1, 2)], cores=(1,), zs=(0,))
    r1 = send(second, pairs(along_z([(0, 1)], (0,), (0,)) + along_z([(0, 3)], (0,), (1,)) + lay_y))
    r2 = send(first, pairs(along_z([(0, 2)], (0,), (1,))))
    c1, c3 = (send(top, along_x([(0, to)])) for to in (1, 3))

    e = jnp.where(y == 0, jnp.stack([e, f]), jnp.stack([f, e]))
    e = jnp.where((x == 0) & (z == 0) & (y < 2), e, 0.0)
    e = e + send(e, pairs(along_z([(0, 1)], ys=(0, 1), xs=plane)))
    e = e + send(e, pairs(along_z([(0, 3), (1, 2)], ys=(0, 1), xs=plane)))
    e = e + send(e, pairs(along_y([(0, 3), (1, 2)], xs=plane)))

    kept = (z == 0) & jnp.where(core == 0, y == 0, y < 2)
    own = jnp.where(kept, first, r1 + r2)
    own = after(own, e)
    lines = [
        pairs(
            along_y([(0, d % 4)], (0,), (0, 1))
            + along_y([(1, (1 + d) % 4)], (0,), (2, 3))
            + along_z([(0, d % 4)], (1,))
        )
        for d in (1, 3, 2)
    ]
    b1, b3, b2 = (send(own, moves) for moves in lines)
    c2 = send(after(c1, c3, e), along_x([(1, 2)]))

    e = after(e, b3)
    e = e + send(e, along_x([(0, 3)]))
    mine = e + send(e, along_x([(0, 1), (3, 2)]))
    g = own + b1 + b2 + b3
    mine = after(mine, g)
    other = send(mine, SWAP)
    around = [
        pairs(
            along_z([(a, (a + d) % 4) for a in SPAN], (0,)) + along_y([(a, (a + d) % 4) for a in SPAN], (1,))
        )
        for d in (1, 3, 2)
    ]
    g1, g3, g2 = (send(g, moves) for moves in around)
    c = jnp.where(x == 0, top, c1 + c2 + c3)
    c = after(c, other)
    lower, inverse = factor_corner(place[2:3], mine, other)
    columns = jnp.stack([c, send(c, SWAP)])
    columns = jnp.where(core == 0, columns, columns[::-1])
    result = update_trailing(place, lower, inverse, (g, g3, g2, g1), columns, m)
    return result.reshape(kernel.shape)


def solution(mesh):
    placed = P(None, "row", None, None, "col", None)
    return jax.shard_map(local, mesh=mesh, in_specs=(placed,), out_specs=placed, check_vma=False)
```

```python
import jax
import jax.numpy as jnp
from jax import lax
from jax.experimental import pallas as pl
from jax.experimental.pallas import tpu as pltpu
from jax.sharding import PartitionSpec as P

F32 = jnp.float32
BF16 = jnp.bfloat16
BOTH = ("row", "col")
NB = 128
W2 = 2 * NB
TR = 256


def split2(x):
    high = x.astype(BF16)
    return high, (x - high.astype(F32)).astype(BF16)


def gram(a, b):
    def split3(x):
        h = x.astype(BF16).astype(F32)
        mid = (x - h).astype(BF16).astype(F32)
        return h, mid, x - h - mid

    ah, am, al = split3(a)
    bh, bm, bl = split3(b)
    lhs = jnp.concatenate([ah, ah, am, ah, al, am], axis=0).astype(BF16)
    rhs = jnp.concatenate([bh, bm, bh, bl, bh, bm], axis=0).astype(BF16)
    return lax.dot_general(lhs, rhs, (((0,), (0,)), ((), ())), preferred_element_type=F32)


def factor_kernel(where_ref, mine_ref, other_ref, lower_ref, inverse_ref, whole_ref, s_ref):
    core = where_ref[0]
    size, sub_rows, group = W2, 8, 32

    def place(first, second):
        s_ref[0:NB, 0:NB] = first[0]
        s_ref[NB:W2, 0:NB] = second[0]
        s_ref[0:NB, NB:W2] = second[0].T
        s_ref[NB:W2, NB:W2] = second[1]

    @pl.when(core == 0)
    def _():
        place(mine_ref, other_ref)

    @pl.when(core == 1)
    def _():
        place(other_ref, mine_ref)

    rows = lax.broadcasted_iota(jnp.int32, (size, size), 0)
    cols = lax.broadcasted_iota(jnp.int32, (size, size), 1)
    s_ref[:, size:] = jnp.where(rows == cols, 1.0, 0.0)
    sub = lax.broadcasted_iota(jnp.int32, (sub_rows, NB), 0)
    tiles = 3
    width = NB * tiles
    panels = group // sub_rows
    for o in range(0, size, group):
        lo = (o // NB) * NB
        r = [
            [
                s_ref[o + sub_rows * q : o + sub_rows * (q + 1), lo + NB * t : lo + NB * (t + 1)]
                for t in range(tiles)
            ]
            for q in range(panels)
        ]
        for p in range(panels):
            oo = o - lo + p * sub_rows
            c = [
                [jnp.broadcast_to(r[q][0][:, oo + j : oo + j + 1], (sub_rows, NB)) for j in range(sub_rows)]
                if q >= p
                else None
                for q in range(panels)
            ]
            b = [
                [
                    jnp.broadcast_to(c[p][j][i : i + 1, :], (sub_rows, NB)) if i >= j else None
                    for j in range(sub_rows)
                ]
                for i in range(sub_rows)
            ]
            scale = None
            for k in range(sub_rows):
                s = lax.rsqrt(b[k][k])
                scale = s if scale is None else jnp.where(sub >= k, s, scale)
                m = [None] * sub_rows
                for i in range(k + 1, sub_rows):
                    m[i] = b[i][k] * s
                for i in range(k + 1, sub_rows):
                    for j in range(k + 1, i + 1):
                        b[i][j] = b[i][j] - m[i] * m[j]
                u = [jnp.broadcast_to(r[p][t][k : k + 1, :], (sub_rows, NB)) * s for t in range(tiles)]
                for q in range(p, panels):
                    mult = c[q][k] * s
                    for j in range(k + 1, sub_rows):
                        c[q][j] = c[q][j] - mult * m[j]
                    if q == p:
                        if k == sub_rows - 1:
                            continue
                        mult = jnp.where(sub > k, mult, 0.0)
                    r[q] = [r[q][t] - mult * u[t] for t in range(tiles)]
            for t in range(tiles):
                s_ref[
                    o + sub_rows * p : o + sub_rows * (p + 1), lo + NB * t : lo + NB * (t + 1)
                ] = r[p][t] * scale
        if o + group < size:
            lo2 = ((o + group) // NB) * NB
            uu = s_ref[o : o + group, lo2 : lo + width]
            left = size - lo2
            update = gram(uu[:, :left], uu)
            skip = o + group - lo2
            s_ref[o + group : size, lo2 : lo + width] = (
                s_ref[o + group : size, lo2 : lo + width] - update[skip:, :]
            )
    lower_ref[...] = jnp.where(cols >= rows, s_ref[:, 0:size], 0.0).T
    inverse = jnp.where(cols <= rows, s_ref[:, size:], 0.0)
    inverse_ref[...] = inverse.T
    whole_ref[...] = gram(inverse, inverse)


def factor_corner(place, mine, other):
    vmem = pl.BlockSpec(memory_space=pltpu.VMEM)
    return pl.pallas_call(
        factor_kernel,
        out_shape=(jax.ShapeDtypeStruct((W2, W2), F32),) * 3,
        in_specs=[pl.BlockSpec(memory_space=pltpu.SMEM), vmem, vmem],
        out_specs=(vmem, vmem, vmem),
        scratch_shapes=[pltpu.VMEM((W2, 2 * W2), F32)],
        compiler_params=pltpu.CompilerParams(vmem_limit_bytes=8 * 1024 * 1024),
        cost_estimate=pl.CostEstimate(flops=8_000_000_000, bytes_accessed=1_000_000, transcendentals=256),
        name="corner_factor",
    )(place, mine, other)


STEPS = 4


def trailing_kernel(
    place_ref, lower_ref, inverse_ref, whole_ref, g_ref, gm_ref, gf_ref, gp_ref, columns_ref, m_ref,
    o_ref, a_ref, old_ref, new_ref, wc_ref, a_sems, m_sems, o_sems,
):
    row, col, core, z, y = (place_ref[n] for n in range(5))
    here = jnp.where(core == 0, z, y)
    pieces = [
        pltpu.make_async_copy(ref, a_ref.at[n], a_sems.at[n])
        for n, ref in enumerate((g_ref, gm_ref, gf_ref, gp_ref))
    ]
    for piece in pieces:
        piece.start()
    loads = [
        pltpu.make_async_copy(
            m_ref.at[2 * s * TR : 2 * (s + 1) * TR], old_ref.at[s], m_sems.at[s]
        )
        for s in range(STEPS)
    ]
    for load in loads:
        load.start()

    high, low = split2(whole_ref[...])
    lhs = jnp.concatenate([high, high, low], axis=1)
    for j in range(0, 8, 2):
        x = jnp.concatenate(
            [
                jnp.concatenate([columns_ref[n, :, jj, :] for n in range(2)], axis=0)
                for jj in (j, j + 1)
            ],
            axis=1,
        )
        xh, xl = split2(x)
        w = jnp.dot(lhs, jnp.concatenate([xh, xl, xh], axis=0), preferred_element_type=F32)
        wh, wl = split2(w)
        span = pl.ds(j * NB, W2)
        wc_ref[0:W2, span] = wh
        wc_ref[W2 : 2 * W2, span] = wl
        wc_ref[2 * W2 : 3 * W2, span] = wh
    for k in range(2):

        @pl.when(col == k)
        def _():
            wh, wl = split2(-inverse_ref[:, k * NB : (k + 1) * NB])
            wc_ref[0:W2, 0:NB] = wh
            wc_ref[W2 : 2 * W2, 0:NB] = wl
            wc_ref[2 * W2 : 3 * W2, 0:NB] = wh

    for piece in pieces:
        piece.wait()

    stores = []
    for s in range(STEPS):
        half = s // 2
        slot0 = (jnp.where(core == 0, half, 3 * half) - here + 4) % 4
        slot1 = (jnp.where(core == 0, 2 + half, 1 + half) - here + 4) % 4
        i = 2 * (s % 2)
        a = jnp.concatenate(
            [a_ref[slot0, i : i + 2].reshape(2 * TR, NB), a_ref[slot1, i : i + 2].reshape(2 * TR, NB)], axis=1
        )
        ah, al = split2(a)
        u = jnp.dot(jnp.concatenate([ah, ah, al], axis=1), wc_ref[...], preferred_element_type=F32)
        loads[s].wait()
        new_ref[s] = old_ref[s] - u.reshape(2 * TR, 8, NB)

        @pl.when(col < 2)
        def _():
            new_ref[s, :, 0, :] = -u[:, 0:NB]

        if s == 0:

            @pl.when(row < 2)
            def _():
                new_ref[s, 0:NB, :, :] = jnp.zeros((NB, 8, NB), F32)

                @pl.when(col < 2)
                def _():
                    new_ref[s, 0:NB, 0, :] = lower_ref[
                        pl.ds(pl.multiple_of(row * NB, NB), NB), pl.ds(pl.multiple_of(col * NB, NB), NB)
                    ]

        store = pltpu.make_async_copy(
            new_ref.at[s], o_ref.at[2 * s * TR : 2 * (s + 1) * TR], o_sems.at[s]
        )
        store.start()
        stores.append(store)
    for store in stores:
        store.wait()


def update_trailing(place, lower, inverse, whole, pieces, columns, m):
    anywhere = pl.BlockSpec(memory_space=pl.ANY)
    vmem = pl.BlockSpec(memory_space=pltpu.VMEM)
    return pl.pallas_call(
        trailing_kernel,
        out_shape=jax.ShapeDtypeStruct(m.shape, F32),
        in_specs=[pl.BlockSpec(memory_space=pltpu.SMEM), vmem, vmem, vmem] + [anywhere] * 4 + [vmem, anywhere],
        out_specs=anywhere,
        scratch_shapes=[
            pltpu.VMEM((4, 4, TR, NB), F32),
            pltpu.VMEM((STEPS, 2 * TR, 8, NB), F32),
            pltpu.VMEM((STEPS, 2 * TR, 8, NB), F32),
            pltpu.VMEM((3 * W2, 8 * NB), BF16),
            pltpu.SemaphoreType.DMA((4,)),
            pltpu.SemaphoreType.DMA((STEPS,)),
            pltpu.SemaphoreType.DMA((STEPS,)),
        ],
        compiler_params=pltpu.CompilerParams(vmem_limit_bytes=36 * 1024 * 1024),
        cost_estimate=pl.CostEstimate(flops=4_000_000_000, bytes_accessed=20_000_000, transcendentals=0),
        name="trailing_update",
    )(place, lower, inverse, whole, *pieces, columns, m)


def device(x, core, z, y):
    return (x % 4 * 2 + core) * 16 + z % 4 * 4 + y % 4


def pairs(moves):
    return [(device(*a), device(*b)) for a, b in moves]


SPAN = range(4)
CORES = range(2)


def along_x(hops):
    return pairs(
        [((a, k, z, y), (b, k, z, y)) for a, b in hops for k in CORES for z in SPAN for y in SPAN]
    )


def along_z(hops, cores=CORES, ys=SPAN, xs=SPAN):
    return [((x, k, a, y), (x, k, b, y)) for a, b in hops for x in xs for k in cores for y in ys]


def along_y(hops, cores=CORES, zs=SPAN, xs=SPAN):
    return [((x, k, z, a), (x, k, z, b)) for a, b in hops for x in xs for k in cores for z in zs]


SWAP = pairs([((x, k, z, y), (x, 1 - k, z, y)) for x in SPAN for k in CORES for z in SPAN for y in SPAN])


def send(value, moves):
    return lax.ppermute(value, BOTH, moves)


def after(value, *others):
    return lax.optimization_barrier((value, *others))[0]


def extract_kernel(place_ref, m_ref, first_ref, second_ref, block_ref, top_ref, sems):
    x, z, y = (place_ref[n] for n in (5, 3, 4))
    top = pltpu.make_async_copy(m_ref.at[0:NB], top_ref, sems.at[9])
    block = pltpu.make_async_copy(m_ref.at[0:NB, 0, :], block_ref, sems.at[8])
    source = (z == 0) & (y < 2)
    corner = source & (x == 0)

    @pl.when(x == 0)
    def _():
        top.start()

    @pl.when(corner)
    def _():
        block.start()

    @pl.when(source)
    def _():
        copies = [
            pltpu.make_async_copy(m_ref.at[TR * n : TR * (n + 1), 0, :], ref.at[n % 4], sems.at[n])
            for n, ref in enumerate([first_ref] * 4 + [second_ref] * 4)
        ]
        for copy in copies:
            copy.start()
        for copy in copies:
            copy.wait()

    @pl.when(corner)
    def _():
        block.wait()

    @pl.when(jnp.logical_not(corner))
    def _():
        block_ref[...] = jnp.zeros((NB, NB), F32)

    @pl.when(x == 0)
    def _():
        top.wait()


def extract(place, m):
    anywhere = pl.BlockSpec(memory_space=pl.ANY)
    half = jax.ShapeDtypeStruct((4, TR, NB), F32)
    return pl.pallas_call(
        extract_kernel,
        out_shape=(half, half, jax.ShapeDtypeStruct((NB, NB), F32), jax.ShapeDtypeStruct((NB, 8, NB), F32)),
        in_specs=[pl.BlockSpec(memory_space=pltpu.SMEM), anywhere],
        out_specs=(anywhere, anywhere, pl.BlockSpec(memory_space=pltpu.VMEM), anywhere),
        scratch_shapes=[pltpu.SemaphoreType.DMA((10,))],
        compiler_params=pltpu.CompilerParams(vmem_limit_bytes=4 * 1024 * 1024),
        cost_estimate=pl.CostEstimate(flops=0, bytes_accessed=4_000_000, transcendentals=0),
        name="extract_panels",
    )(place, m)


def local(kernel):
    row = lax.axis_index("row")
    col = lax.axis_index("col")
    x, core, z, y = row // 2, row % 2, col // 4, col % 4
    place = jnp.stack([row, col, core, z, y, x]).astype(jnp.int32)
    m = kernel.reshape(16 * NB, 8, NB)
    m = pltpu.with_memory_space_constraint(m, pltpu.HBM)
    first, second, e, top = extract(place, m)

    plane = (0,)
    f = send(e, pairs(along_y([(0, 1), (1, 0)], xs=plane, zs=(0,))))

    lay_y = along_y([(0, 3), (1, 2)], cores=(1,), zs=(0,))
    r1 = send(second, pairs(along_z([(0, 1)], (0,), (0,)) + along_z([(0, 3)], (0,), (1,)) + lay_y))
    r2 = send(first, pairs(along_z([(0, 2)], (0,), (1,))))
    c1, c3 = (send(top, along_x([(0, to)])) for to in (1, 3))

    e = jnp.where(y == 0, jnp.stack([e, f]), jnp.stack([f, e]))
    e = jnp.where((x == 0) & (z == 0) & (y < 2), e, 0.0)
    e = e + send(e, pairs(along_z([(0, 1)], ys=(0, 1), xs=plane)))
    e = e + send(e, pairs(along_z([(0, 3), (1, 2)], ys=(0, 1), xs=plane)))
    e = e + send(e, pairs(along_y([(0, 3), (1, 2)], xs=plane)))

    kept = (z == 0) & jnp.where(core == 0, y == 0, y < 2)
    own = jnp.where(kept, first, r1 + r2)
    own = after(own, e)
    lines = [
        pairs(
            along_y([(0, d % 4)], (0,), (0, 1))
            + along_y([(1, (1 + d) % 4)], (0,), (2, 3))
            + along_z([(0, d % 4)], (1,))
        )
        for d in (1, 3, 2)
    ]
    b1, b3, b2 = (send(own, moves) for moves in lines)
    c2 = send(after(c1, c3, e), along_x([(1, 2)]))

    e = after(e, b3)
    e = e + send(e, along_x([(0, 3)]))
    mine = e + send(e, along_x([(0, 1), (3, 2)]))
    g = own + b1 + b2 + b3
    mine = after(mine, g)
    other = send(mine, SWAP)
    around = [
        pairs(
            along_z([(a, (a + d) % 4) for a in SPAN], (0,)) + along_y([(a, (a + d) % 4) for a in SPAN], (1,))
        )
        for d in (1, 3, 2)
    ]
    g1, g3, g2 = (send(g, moves) for moves in around)
    c = jnp.where(x == 0, top, c1 + c2 + c3)
    c = after(c, other)
    lower, inverse, whole = factor_corner(place[2:3], mine, other)
    columns = jnp.stack([c, send(c, SWAP)])
    columns = jnp.where(core == 0, columns, columns[::-1])
    result = update_trailing(place, lower, inverse, whole, (g, g3, g2, g1), columns, m)
    return result.reshape(kernel.shape)


def solution(mesh):
    placed = P(None, "row", None, None, "col", None)
    return jax.shard_map(local, mesh=mesh, in_specs=(placed,), out_specs=placed, check_vma=False)
```

```python
import jax
import jax.numpy as jnp
from jax import lax
from jax.experimental import pallas as pl
from jax.experimental.pallas import tpu as pltpu
from jax.sharding import PartitionSpec as P

F32 = jnp.float32
BF16 = jnp.bfloat16
BOTH = ("row", "col")
NB = 128
W2 = 2 * NB
TR = 256


def split2(x):
    high = x.astype(BF16)
    return high, (x - high.astype(F32)).astype(BF16)


def gram(a, b):
    def split3(x):
        h = x.astype(BF16).astype(F32)
        mid = (x - h).astype(BF16).astype(F32)
        return h, mid, x - h - mid

    ah, am, al = split3(a)
    bh, bm, bl = split3(b)
    lhs = jnp.concatenate([ah, ah, am, ah, al, am], axis=0).astype(BF16)
    rhs = jnp.concatenate([bh, bm, bh, bl, bh, bm], axis=0).astype(BF16)
    return lax.dot_general(lhs, rhs, (((0,), (0,)), ((), ())), preferred_element_type=F32)


def factor_kernel(where_ref, mine_ref, other_ref, lower_ref, inverse_ref, whole_ref, s_ref):
    core = where_ref[0]
    size, sub_rows, group = W2, 8, 32

    def place(first, second):
        s_ref[0:NB, 0:NB] = first[0]
        s_ref[NB:W2, 0:NB] = second[0]
        s_ref[0:NB, NB:W2] = second[0].T
        s_ref[NB:W2, NB:W2] = second[1]

    @pl.when(core == 0)
    def _():
        place(mine_ref, other_ref)

    @pl.when(core == 1)
    def _():
        place(other_ref, mine_ref)

    rows = lax.broadcasted_iota(jnp.int32, (size, size), 0)
    cols = lax.broadcasted_iota(jnp.int32, (size, size), 1)
    s_ref[:, size:] = jnp.where(rows == cols, 1.0, 0.0)
    sub = lax.broadcasted_iota(jnp.int32, (sub_rows, NB), 0)
    tiles = 3
    width = NB * tiles
    panels = group // sub_rows
    for o in range(0, size, group):
        lo = (o // NB) * NB
        r = [
            [
                s_ref[o + sub_rows * q : o + sub_rows * (q + 1), lo + NB * t : lo + NB * (t + 1)]
                for t in range(tiles)
            ]
            for q in range(panels)
        ]
        for p in range(panels):
            oo = o - lo + p * sub_rows
            c = [
                [jnp.broadcast_to(r[q][0][:, oo + j : oo + j + 1], (sub_rows, NB)) for j in range(sub_rows)]
                if q >= p
                else None
                for q in range(panels)
            ]
            b = [
                [
                    jnp.broadcast_to(c[p][j][i : i + 1, :], (sub_rows, NB)) if i >= j else None
                    for j in range(sub_rows)
                ]
                for i in range(sub_rows)
            ]
            scale = None
            for k in range(sub_rows):
                s = lax.rsqrt(b[k][k])
                scale = s if scale is None else jnp.where(sub >= k, s, scale)
                m = [None] * sub_rows
                for i in range(k + 1, sub_rows):
                    m[i] = b[i][k] * s
                for i in range(k + 1, sub_rows):
                    for j in range(k + 1, i + 1):
                        b[i][j] = b[i][j] - m[i] * m[j]
                u = [jnp.broadcast_to(r[p][t][k : k + 1, :], (sub_rows, NB)) * s for t in range(tiles)]
                for q in range(p, panels):
                    mult = c[q][k] * s
                    for j in range(k + 1, sub_rows):
                        c[q][j] = c[q][j] - mult * m[j]
                    if q == p:
                        if k == sub_rows - 1:
                            continue
                        mult = jnp.where(sub > k, mult, 0.0)
                    r[q] = [r[q][t] - mult * u[t] for t in range(tiles)]
            for t in range(tiles):
                s_ref[
                    o + sub_rows * p : o + sub_rows * (p + 1), lo + NB * t : lo + NB * (t + 1)
                ] = r[p][t] * scale
        if o + group < size:
            lo2 = ((o + group) // NB) * NB
            uu = s_ref[o : o + group, lo2 : lo + width]
            left = size - lo2
            update = gram(uu[:, :left], uu)
            skip = o + group - lo2
            s_ref[o + group : size, lo2 : lo + width] = (
                s_ref[o + group : size, lo2 : lo + width] - update[skip:, :]
            )
    lower_ref[...] = jnp.where(cols >= rows, s_ref[:, 0:size], 0.0).T
    inverse = jnp.where(cols <= rows, s_ref[:, size:], 0.0)
    inverse_ref[...] = inverse.T
    whole_ref[...] = gram(inverse, inverse)


def factor_corner(place, mine, other):
    vmem = pl.BlockSpec(memory_space=pltpu.VMEM)
    return pl.pallas_call(
        factor_kernel,
        out_shape=(jax.ShapeDtypeStruct((W2, W2), F32),) * 3,
        in_specs=[pl.BlockSpec(memory_space=pltpu.SMEM), vmem, vmem],
        out_specs=(vmem, vmem, vmem),
        scratch_shapes=[pltpu.VMEM((W2, 2 * W2), F32)],
        compiler_params=pltpu.CompilerParams(vmem_limit_bytes=8 * 1024 * 1024),
        cost_estimate=pl.CostEstimate(flops=8_000_000_000, bytes_accessed=1_000_000, transcendentals=256),
        name="corner_factor",
    )(place, mine, other)


STEPS = ((0, 2), (2, 4), (4, 6), (6, 7), (7, 8))


def trailing_kernel(
    place_ref, lower_ref, inverse_ref, whole_ref, g_ref, gm_ref, gf_ref, gp_ref, columns_ref, m_ref,
    o_ref, a_ref, old_ref, new_ref, wc_ref, a_sems, m_sems, o_sems,
):
    row, col, core, z, y = (place_ref[n] for n in range(5))
    here = jnp.where(core == 0, z, y)
    pieces = [
        pltpu.make_async_copy(ref, a_ref.at[n], a_sems.at[n])
        for n, ref in enumerate((g_ref, gm_ref, gf_ref, gp_ref))
    ]
    for piece in pieces:
        piece.start()
    loads = [
        pltpu.make_async_copy(m_ref.at[i * TR : j * TR], old_ref.at[i * TR : j * TR], m_sems.at[n])
        for n, (i, j) in enumerate(STEPS)
    ]
    for load in loads:
        load.start()

    high, low = split2(whole_ref[...])
    lhs = jnp.concatenate([high, high, low], axis=1)
    for j in range(0, 8, 2):
        x = jnp.concatenate(
            [
                jnp.concatenate([columns_ref[n, :, jj, :] for n in range(2)], axis=0)
                for jj in (j, j + 1)
            ],
            axis=1,
        )
        xh, xl = split2(x)
        w = jnp.dot(lhs, jnp.concatenate([xh, xl, xh], axis=0), preferred_element_type=F32)
        wh, wl = split2(w)
        span = pl.ds(j * NB, W2)
        wc_ref[0:W2, span] = wh
        wc_ref[W2 : 2 * W2, span] = wl
        wc_ref[2 * W2 : 3 * W2, span] = wh
    for k in range(2):

        @pl.when(col == k)
        def _():
            wh, wl = split2(-inverse_ref[:, k * NB : (k + 1) * NB])
            wc_ref[0:W2, 0:NB] = wh
            wc_ref[W2 : 2 * W2, 0:NB] = wl
            wc_ref[2 * W2 : 3 * W2, 0:NB] = wh

    for piece in pieces:
        piece.wait()

    stores = []
    for n, (first, last) in enumerate(STEPS):
        half = first // 4
        slot0 = (jnp.where(core == 0, half, 3 * half) - here + 4) % 4
        slot1 = (jnp.where(core == 0, 2 + half, 1 + half) - here + 4) % 4
        span = pl.ds(first % 4, last - first)
        count = (last - first) * TR
        a = jnp.concatenate(
            [a_ref[slot0, span].reshape(count, NB), a_ref[slot1, span].reshape(count, NB)], axis=1
        )
        ah, al = split2(a)
        u = jnp.dot(jnp.concatenate([ah, ah, al], axis=1), wc_ref[...], preferred_element_type=F32)
        loads[n].wait()
        span = pl.ds(first * TR, count)
        new_ref[span] = old_ref[span] - u.reshape(count, 8, NB)

        @pl.when(col < 2)
        def _():
            new_ref[span, 0, :] = -u[:, 0:NB]

        if n == 0:

            @pl.when(row < 2)
            def _():
                new_ref[0:NB, :, :] = jnp.zeros((NB, 8, NB), F32)

                @pl.when(col < 2)
                def _():
                    new_ref[0:NB, 0, :] = lower_ref[
                        pl.ds(pl.multiple_of(row * NB, NB), NB), pl.ds(pl.multiple_of(col * NB, NB), NB)
                    ]

        store = pltpu.make_async_copy(new_ref.at[span], o_ref.at[span], o_sems.at[n])
        store.start()
        stores.append(store)
    for store in stores:
        store.wait()


def update_trailing(place, lower, inverse, whole, pieces, columns, m):
    anywhere = pl.BlockSpec(memory_space=pl.ANY)
    vmem = pl.BlockSpec(memory_space=pltpu.VMEM)
    return pl.pallas_call(
        trailing_kernel,
        out_shape=jax.ShapeDtypeStruct(m.shape, F32),
        in_specs=[pl.BlockSpec(memory_space=pltpu.SMEM), vmem, vmem, vmem] + [anywhere] * 4 + [vmem, anywhere],
        out_specs=anywhere,
        scratch_shapes=[
            pltpu.VMEM((4, 4, TR, NB), F32),
            pltpu.VMEM(m.shape, F32),
            pltpu.VMEM(m.shape, F32),
            pltpu.VMEM((3 * W2, 8 * NB), BF16),
            pltpu.SemaphoreType.DMA((4,)),
            pltpu.SemaphoreType.DMA((len(STEPS),)),
            pltpu.SemaphoreType.DMA((len(STEPS),)),
        ],
        compiler_params=pltpu.CompilerParams(vmem_limit_bytes=36 * 1024 * 1024),
        cost_estimate=pl.CostEstimate(flops=4_000_000_000, bytes_accessed=20_000_000, transcendentals=0),
        name="trailing_update",
    )(place, lower, inverse, whole, *pieces, columns, m)


def device(x, core, z, y):
    return (x % 4 * 2 + core) * 16 + z % 4 * 4 + y % 4


def pairs(moves):
    return [(device(*a), device(*b)) for a, b in moves]


SPAN = range(4)
CORES = range(2)


def along_x(hops):
    return pairs(
        [((a, k, z, y), (b, k, z, y)) for a, b in hops for k in CORES for z in SPAN for y in SPAN]
    )


def along_z(hops, cores=CORES, ys=SPAN, xs=SPAN):
    return [((x, k, a, y), (x, k, b, y)) for a, b in hops for x in xs for k in cores for y in ys]


def along_y(hops, cores=CORES, zs=SPAN, xs=SPAN):
    return [((x, k, z, a), (x, k, z, b)) for a, b in hops for x in xs for k in cores for z in zs]


SWAP = pairs([((x, k, z, y), (x, 1 - k, z, y)) for x in SPAN for k in CORES for z in SPAN for y in SPAN])


def send(value, moves):
    return lax.ppermute(value, BOTH, moves)


def after(value, *others):
    return lax.optimization_barrier((value, *others))[0]


def extract_kernel(place_ref, m_ref, first_ref, second_ref, block_ref, top_ref, sems):
    x, z, y = (place_ref[n] for n in (5, 3, 4))
    top = pltpu.make_async_copy(m_ref.at[0:NB], top_ref, sems.at[9])
    block = pltpu.make_async_copy(m_ref.at[0:NB, 0, :], block_ref, sems.at[8])
    source = (z == 0) & (y < 2)
    corner = source & (x == 0)

    @pl.when(x == 0)
    def _():
        top.start()

    @pl.when(corner)
    def _():
        block.start()

    @pl.when(source)
    def _():
        copies = [
            pltpu.make_async_copy(m_ref.at[TR * n : TR * (n + 1), 0, :], ref.at[n % 4], sems.at[n])
            for n, ref in enumerate([first_ref] * 4 + [second_ref] * 4)
        ]
        for copy in copies:
            copy.start()
        for copy in copies:
            copy.wait()

    @pl.when(corner)
    def _():
        block.wait()

    @pl.when(jnp.logical_not(corner))
    def _():
        block_ref[...] = jnp.zeros((NB, NB), F32)

    @pl.when(x == 0)
    def _():
        top.wait()


def extract(place, m):
    anywhere = pl.BlockSpec(memory_space=pl.ANY)
    half = jax.ShapeDtypeStruct((4, TR, NB), F32)
    return pl.pallas_call(
        extract_kernel,
        out_shape=(half, half, jax.ShapeDtypeStruct((NB, NB), F32), jax.ShapeDtypeStruct((NB, 8, NB), F32)),
        in_specs=[pl.BlockSpec(memory_space=pltpu.SMEM), anywhere],
        out_specs=(anywhere, anywhere, pl.BlockSpec(memory_space=pltpu.VMEM), anywhere),
        scratch_shapes=[pltpu.SemaphoreType.DMA((10,))],
        compiler_params=pltpu.CompilerParams(vmem_limit_bytes=4 * 1024 * 1024),
        cost_estimate=pl.CostEstimate(flops=0, bytes_accessed=4_000_000, transcendentals=0),
        name="extract_panels",
    )(place, m)


def local(kernel):
    row = lax.axis_index("row")
    col = lax.axis_index("col")
    x, core, z, y = row // 2, row % 2, col // 4, col % 4
    place = jnp.stack([row, col, core, z, y, x]).astype(jnp.int32)
    m = kernel.reshape(16 * NB, 8, NB)
    m = pltpu.with_memory_space_constraint(m, pltpu.HBM)
    first, second, e, top = extract(place, m)

    f = send(e, pairs(along_y([(0, 1), (1, 0)], xs=(0,), zs=(0,))))
    e = jnp.where(y == 0, jnp.stack([e, f]), jnp.stack([f, e]))
    e = jnp.where((x == 0) & (z == 0) & (y < 2), e, 0.0)
    x3, x1, x2 = (send(e, along_x([(0, to)])) for to in (3, 1, 2))
    e = e + x1 + x2 + x3

    lay_y = along_y([(0, 3), (1, 2)], cores=(1,), zs=(0,))
    near = pairs(along_z([(0, 1)], (0,), (0,)) + along_z([(0, 3)], (0,), (1,)) + lay_y)
    far = pairs(along_z([(0, 2)], (0,), (1,)))
    r1, r2 = send(second, near), send(first, far)
    e1, e2 = send(e, near), send(e, far)

    kept = (z == 0) & jnp.where(core == 0, y == 0, y < 2)
    own = jnp.concatenate(
        [jnp.where(kept, first, r1 + r2).reshape(8, NB, NB), jnp.where(kept, e, e1 + e2)]
    )
    lines = [
        pairs(
            along_y([(0, d % 4)], (0,), (0, 1))
            + along_y([(1, (1 + d) % 4)], (0,), (2, 3))
            + along_z([(0, d % 4)], (1,))
        )
        for d in (1, 3, 2)
    ]
    b1, b3, b2 = (send(own, moves) for moves in lines)
    top = after(top, own)
    c1, c3 = (send(top, along_x([(0, to)])) for to in (1, 3))
    c2 = send(c1, along_x([(1, 2)]))
    g = own + b1 + b2 + b3
    e, g = g[8:], g[:8].reshape(4, TR, NB)

    mine = e
    other = send(mine, SWAP)
    g = after(g, other)
    around = [
        pairs(
            along_z([(a, (a + d) % 4) for a in SPAN], (0,)) + along_y([(a, (a + d) % 4) for a in SPAN], (1,))
        )
        for d in (1, 3, 2)
    ]
    g1, g3, g2 = (send(g, moves) for moves in around)
    c = jnp.where(x == 0, top, c1 + c2 + c3)
    lower, inverse, whole = factor_corner(place[2:3], mine, other)
    columns = jnp.stack([c, send(c, SWAP)])
    columns = jnp.where(core == 0, columns, columns[::-1])
    result = update_trailing(place, lower, inverse, whole, (g, g3, g2, g1), columns, m)
    return result.reshape(kernel.shape)


def solution(mesh):
    placed = P(None, "row", None, None, "col", None)
    return jax.shard_map(local, mesh=mesh, in_specs=(placed,), out_specs=placed, check_vma=False)
```

```python
import jax
import jax.numpy as jnp
from jax import lax
from jax.experimental import pallas as pl
from jax.experimental.pallas import tpu as pltpu
from jax.sharding import PartitionSpec as P

F32 = jnp.float32
BF16 = jnp.bfloat16
BOTH = ("row", "col")
NB = 128
W2 = 2 * NB
TR = 256


def split2(x):
    high = x.astype(BF16)
    return high, (x - high.astype(F32)).astype(BF16)


def gram(a, b):
    def split3(x):
        h = x.astype(BF16).astype(F32)
        mid = (x - h).astype(BF16).astype(F32)
        return h, mid, x - h - mid

    ah, am, al = split3(a)
    bh, bm, bl = split3(b)
    lhs = jnp.concatenate([ah, ah, am, ah, al, am], axis=0).astype(BF16)
    rhs = jnp.concatenate([bh, bm, bh, bl, bh, bm], axis=0).astype(BF16)
    return lax.dot_general(lhs, rhs, (((0,), (0,)), ((), ())), preferred_element_type=F32)


def factor_kernel(where_ref, mine_ref, other_ref, lower_ref, inverse_ref, whole_ref, s_ref):
    core = where_ref[0]
    size, sub_rows, group = W2, 8, 32

    def place(first, second):
        s_ref[0:NB, 0:NB] = first[0]
        s_ref[NB:W2, 0:NB] = second[0]
        s_ref[0:NB, NB:W2] = second[0].T
        s_ref[NB:W2, NB:W2] = second[1]

    @pl.when(core == 0)
    def _():
        place(mine_ref, other_ref)

    @pl.when(core == 1)
    def _():
        place(other_ref, mine_ref)

    rows = lax.broadcasted_iota(jnp.int32, (size, size), 0)
    cols = lax.broadcasted_iota(jnp.int32, (size, size), 1)
    s_ref[:, size:] = jnp.where(rows == cols, 1.0, 0.0)
    sub = lax.broadcasted_iota(jnp.int32, (sub_rows, NB), 0)
    tiles = 3
    width = NB * tiles
    panels = group // sub_rows
    for o in range(0, size, group):
        lo = (o // NB) * NB
        r = [
            [
                s_ref[o + sub_rows * q : o + sub_rows * (q + 1), lo + NB * t : lo + NB * (t + 1)]
                for t in range(tiles)
            ]
            for q in range(panels)
        ]
        for p in range(panels):
            oo = o - lo + p * sub_rows
            c = [
                [jnp.broadcast_to(r[q][0][:, oo + j : oo + j + 1], (sub_rows, NB)) for j in range(sub_rows)]
                if q >= p
                else None
                for q in range(panels)
            ]
            b = [
                [
                    jnp.broadcast_to(c[p][j][i : i + 1, :], (sub_rows, NB)) if i >= j else None
                    for j in range(sub_rows)
                ]
                for i in range(sub_rows)
            ]
            scale = None
            for k in range(sub_rows):
                s = lax.rsqrt(b[k][k])
                scale = s if scale is None else jnp.where(sub >= k, s, scale)
                m = [None] * sub_rows
                for i in range(k + 1, sub_rows):
                    m[i] = b[i][k] * s
                for i in range(k + 1, sub_rows):
                    for j in range(k + 1, i + 1):
                        b[i][j] = b[i][j] - m[i] * m[j]
                u = [jnp.broadcast_to(r[p][t][k : k + 1, :], (sub_rows, NB)) * s for t in range(tiles)]
                for q in range(p, panels):
                    mult = c[q][k] * s
                    for j in range(k + 1, sub_rows):
                        c[q][j] = c[q][j] - mult * m[j]
                    if q == p:
                        if k == sub_rows - 1:
                            continue
                        mult = jnp.where(sub > k, mult, 0.0)
                    r[q] = [r[q][t] - mult * u[t] for t in range(tiles)]
            for t in range(tiles):
                s_ref[
                    o + sub_rows * p : o + sub_rows * (p + 1), lo + NB * t : lo + NB * (t + 1)
                ] = r[p][t] * scale
        if o + group < size:
            lo2 = ((o + group) // NB) * NB
            uu = s_ref[o : o + group, lo2 : lo + width]
            left = size - lo2
            update = gram(uu[:, :left], uu)
            skip = o + group - lo2
            s_ref[o + group : size, lo2 : lo + width] = (
                s_ref[o + group : size, lo2 : lo + width] - update[skip:, :]
            )
    lower_ref[...] = jnp.where(cols >= rows, s_ref[:, 0:size], 0.0).T
    inverse = jnp.where(cols <= rows, s_ref[:, size:], 0.0)
    inverse_ref[...] = inverse.T
    whole_ref[...] = gram(inverse, inverse)


def factor_corner(place, mine, other):
    vmem = pl.BlockSpec(memory_space=pltpu.VMEM)
    return pl.pallas_call(
        factor_kernel,
        out_shape=(jax.ShapeDtypeStruct((W2, W2), F32),) * 3,
        in_specs=[pl.BlockSpec(memory_space=pltpu.SMEM), vmem, vmem],
        out_specs=(vmem, vmem, vmem),
        scratch_shapes=[pltpu.VMEM((W2, 2 * W2), F32)],
        compiler_params=pltpu.CompilerParams(vmem_limit_bytes=8 * 1024 * 1024),
        cost_estimate=pl.CostEstimate(flops=8_000_000_000, bytes_accessed=1_000_000, transcendentals=256),
        name="corner_factor",
    )(place, mine, other)


STEPS = ((0, 2), (2, 4), (4, 6), (6, 7), (7, 8))


def trailing_kernel(
    place_ref, lower_ref, inverse_ref, whole_ref, g_ref, gm_ref, gf_ref, gp_ref, columns_ref, m_ref,
    o_ref, a_ref, old_ref, new_ref, wc_ref, a_sems, m_sems, o_sems,
):
    row, col, core, z, y = (place_ref[n] for n in range(5))
    here = jnp.where(core == 0, z, y)
    pieces = [
        pltpu.make_async_copy(ref, a_ref.at[n], a_sems.at[n])
        for n, ref in enumerate((g_ref, gm_ref, gf_ref, gp_ref))
    ]
    for piece in pieces:
        piece.start()
    loads = [
        pltpu.make_async_copy(m_ref.at[i * TR : j * TR], old_ref.at[i * TR : j * TR], m_sems.at[n])
        for n, (i, j) in enumerate(STEPS)
    ]
    for load in loads:
        load.start()

    high, low = split2(whole_ref[...])
    lhs = jnp.concatenate([high, high, low], axis=1)
    for j in range(0, 8, 2):
        x = jnp.concatenate(
            [
                jnp.concatenate([columns_ref[n, :, jj, :] for n in range(2)], axis=0)
                for jj in (j, j + 1)
            ],
            axis=1,
        )
        xh, xl = split2(x)
        w = jnp.dot(lhs, jnp.concatenate([xh, xl, xh], axis=0), preferred_element_type=F32)
        wh, wl = split2(w)
        span = pl.ds(j * NB, W2)
        wc_ref[0:W2, span] = wh
        wc_ref[W2 : 2 * W2, span] = wl
        wc_ref[2 * W2 : 3 * W2, span] = wh
    for k in range(2):

        @pl.when(col == k)
        def _():
            wh, wl = split2(-inverse_ref[:, k * NB : (k + 1) * NB])
            wc_ref[0:W2, 0:NB] = wh
            wc_ref[W2 : 2 * W2, 0:NB] = wl
            wc_ref[2 * W2 : 3 * W2, 0:NB] = wh

    for piece in pieces:
        piece.wait()

    stores = []
    for n, (first, last) in enumerate(STEPS):
        half = first // 4
        slot0 = (jnp.where(core == 0, half, 3 * half) - here + 4) % 4
        slot1 = (jnp.where(core == 0, 2 + half, 1 + half) - here + 4) % 4
        span = pl.ds(first % 4, last - first)
        count = (last - first) * TR
        a = jnp.concatenate(
            [a_ref[slot0, span].reshape(count, NB), a_ref[slot1, span].reshape(count, NB)], axis=1
        )
        ah, al = split2(a)
        u = jnp.dot(jnp.concatenate([ah, ah, al], axis=1), wc_ref[...], preferred_element_type=F32)
        loads[n].wait()
        span = pl.ds(first * TR, count)
        new_ref[span] = old_ref[span] - u.reshape(count, 8, NB)

        @pl.when(col < 2)
        def _():
            new_ref[span, 0, :] = -u[:, 0:NB]

        if n == 0:

            @pl.when(row < 2)
            def _():
                new_ref[0:NB, :, :] = jnp.zeros((NB, 8, NB), F32)

                @pl.when(col < 2)
                def _():
                    new_ref[0:NB, 0, :] = lower_ref[
                        pl.ds(pl.multiple_of(row * NB, NB), NB), pl.ds(pl.multiple_of(col * NB, NB), NB)
                    ]

        store = pltpu.make_async_copy(new_ref.at[span], o_ref.at[span], o_sems.at[n])
        store.start()
        stores.append(store)
    for store in stores:
        store.wait()


def update_trailing(place, lower, inverse, whole, pieces, columns, m):
    anywhere = pl.BlockSpec(memory_space=pl.ANY)
    vmem = pl.BlockSpec(memory_space=pltpu.VMEM)
    return pl.pallas_call(
        trailing_kernel,
        out_shape=jax.ShapeDtypeStruct(m.shape, F32),
        in_specs=[pl.BlockSpec(memory_space=pltpu.SMEM), vmem, vmem, vmem] + [anywhere] * 4 + [vmem, anywhere],
        out_specs=anywhere,
        scratch_shapes=[
            pltpu.VMEM((4, 4, TR, NB), F32),
            pltpu.VMEM(m.shape, F32),
            pltpu.VMEM(m.shape, F32),
            pltpu.VMEM((3 * W2, 8 * NB), BF16),
            pltpu.SemaphoreType.DMA((4,)),
            pltpu.SemaphoreType.DMA((len(STEPS),)),
            pltpu.SemaphoreType.DMA((len(STEPS),)),
        ],
        compiler_params=pltpu.CompilerParams(vmem_limit_bytes=36 * 1024 * 1024),
        cost_estimate=pl.CostEstimate(flops=4_000_000_000, bytes_accessed=20_000_000, transcendentals=0),
        name="trailing_update",
    )(place, lower, inverse, whole, *pieces, columns, m)


def device(x, core, z, y):
    return (x % 4 * 2 + core) * 16 + z % 4 * 4 + y % 4


def pairs(moves):
    return [(device(*a), device(*b)) for a, b in moves]


SPAN = range(4)
CORES = range(2)


def along_x(hops):
    return pairs(
        [((a, k, z, y), (b, k, z, y)) for a, b in hops for k in CORES for z in SPAN for y in SPAN]
    )


def along_z(hops, cores=CORES, ys=SPAN, xs=SPAN):
    return [((x, k, a, y), (x, k, b, y)) for a, b in hops for x in xs for k in cores for y in ys]


def along_y(hops, cores=CORES, zs=SPAN, xs=SPAN):
    return [((x, k, z, a), (x, k, z, b)) for a, b in hops for x in xs for k in cores for z in zs]


SWAP = pairs([((x, k, z, y), (x, 1 - k, z, y)) for x in SPAN for k in CORES for z in SPAN for y in SPAN])


def send(value, moves):
    return lax.ppermute(value, BOTH, moves)


def after(value, *others):
    return lax.optimization_barrier((value, *others))[0]


def extract_kernel(place_ref, m_ref, first_ref, second_ref, block_ref, top_ref, sems):
    x, z, y = (place_ref[n] for n in (5, 3, 4))
    top = pltpu.make_async_copy(m_ref.at[0:NB], top_ref, sems.at[9])
    block = pltpu.make_async_copy(m_ref.at[0:NB, 0, :], block_ref, sems.at[8])
    source = (z == 0) & (y < 2)
    corner = source & (x == 0)

    @pl.when(x == 0)
    def _():
        top.start()

    @pl.when(corner)
    def _():
        block.start()

    @pl.when(source)
    def _():
        copies = [
            pltpu.make_async_copy(m_ref.at[TR * n : TR * (n + 1), 0, :], ref.at[n % 4], sems.at[n])
            for n, ref in enumerate([first_ref] * 4 + [second_ref] * 4)
        ]
        for copy in copies:
            copy.start()
        for copy in copies:
            copy.wait()

    @pl.when(corner)
    def _():
        block.wait()

    @pl.when(jnp.logical_not(corner))
    def _():
        block_ref[...] = jnp.zeros((NB, NB), F32)

    @pl.when(x == 0)
    def _():
        top.wait()


def extract(place, m):
    anywhere = pl.BlockSpec(memory_space=pl.ANY)
    half = jax.ShapeDtypeStruct((4, TR, NB), F32)
    return pl.pallas_call(
        extract_kernel,
        out_shape=(half, half, jax.ShapeDtypeStruct((NB, NB), F32), jax.ShapeDtypeStruct((NB, 8, NB), F32)),
        in_specs=[pl.BlockSpec(memory_space=pltpu.SMEM), anywhere],
        out_specs=(anywhere, anywhere, pl.BlockSpec(memory_space=pltpu.VMEM), anywhere),
        scratch_shapes=[pltpu.SemaphoreType.DMA((10,))],
        compiler_params=pltpu.CompilerParams(vmem_limit_bytes=4 * 1024 * 1024),
        cost_estimate=pl.CostEstimate(flops=0, bytes_accessed=4_000_000, transcendentals=0),
        name="extract_panels",
    )(place, m)


def local(kernel):
    row = lax.axis_index("row")
    col = lax.axis_index("col")
    x, core, z, y = row // 2, row % 2, col // 4, col % 4
    place = jnp.stack([row, col, core, z, y, x]).astype(jnp.int32)
    m = kernel.reshape(16 * NB, 8, NB)
    m = pltpu.with_memory_space_constraint(m, pltpu.HBM)
    first, second, e, top = extract(place, m)

    f = send(e, pairs(along_y([(0, 1), (1, 0)], xs=(0,), zs=(0,))))
    e = jnp.where(y == 0, jnp.stack([e, f]), jnp.stack([f, e]))
    e = jnp.where((x == 0) & (z == 0) & (y < 2), e, 0.0)
    x3, x1, x2 = (send(e, along_x([(0, to)])) for to in (3, 1, 2))
    e = e + x1 + x2 + x3

    lay_y = along_y([(0, 3), (1, 2)], cores=(1,), zs=(0,))
    near = pairs(along_z([(0, 1)], (0,), (0,)) + along_z([(0, 3)], (0,), (1,)) + lay_y)
    far = pairs(along_z([(0, 2)], (0,), (1,)))
    r1, r2 = send(second, near), send(first, far)
    e1, e2 = send(e, near), send(e, far)

    kept = (z == 0) & jnp.where(core == 0, y == 0, y < 2)
    own = jnp.concatenate(
        [jnp.where(kept, first, r1 + r2).reshape(8, NB, NB), jnp.where(kept, e, e1 + e2)]
    )
    lines = [
        pairs(
            along_y([(0, d % 4)], (0,), (0, 1))
            + along_y([(1, (1 + d) % 4)], (0,), (2, 3))
            + along_z([(0, d % 4)], (1,))
        )
        for d in (1, 3, 2)
    ]
    b1, b3, b2 = (send(own, moves) for moves in lines)
    top = after(top, own)
    c = jnp.where(x == 0, top, send(top, along_x([(0, 1)])))
    c2 = send(c, along_x([(0, 3), (1, 2)]))
    g = own + b1 + b2 + b3
    e, g = g[8:], g[:8].reshape(4, TR, NB)

    mine = e
    other = send(mine, SWAP)
    g = after(g, other)
    around = [
        pairs(
            along_z([(a, (a + d) % 4) for a in SPAN], (0,)) + along_y([(a, (a + d) % 4) for a in SPAN], (1,))
        )
        for d in (1, 3, 2)
    ]
    g1, g3, g2 = (send(g, moves) for moves in around)
    c = jnp.where(x < 2, c, c2)
    lower, inverse, whole = factor_corner(place[2:3], mine, other)
    columns = jnp.stack([c, send(c, SWAP)])
    columns = jnp.where(core == 0, columns, columns[::-1])
    result = update_trailing(place, lower, inverse, whole, (g, g3, g2, g1), columns, m)
    return result.reshape(kernel.shape)


def solution(mesh):
    placed = P(None, "row", None, None, "col", None)
    return jax.shard_map(local, mesh=mesh, in_specs=(placed,), out_specs=placed, check_vma=False)
```
